32 devices in a mesh: wave: 4 (over y, x), strip: 8 (over z, core).
Axes of the slice: x: 2, y: 2, z: 4, core: 2. Of those that a mesh axis runs over, the one named last changes fastest.
Arguments:
- unit_params: float32 [9, 8, 24576], P(None, 'strip', 'wave'), may hold values from 0 to 1
- observed: bfloat16 [4, 256, 768, 256], P(None, 'wave', 'strip'), may hold values from -3 to 3
- psf_rows: bfloat16 [256, 4, 65], P('wave'), may hold values from -0.75 to 0.75
- psf_cols: bfloat16 [256, 4, 65], P('wave'), may hold values from -0.75 to 0.75
- pixel_mask: int32 [768, 256], P('strip'), may hold values 0 or 1
- strip_lengths: int32 [8], P('strip'), may hold values from 32 to 96, as said below
Outputs:
- param_grad: float32 [9, 8, 24576], P(None, 'strip', 'wave')
The draws below stay inside these ranges and needn't reach their ends.
Inputs may be any that keep to these rules, and one draw needn't show every extreme that they name: `strip_lengths`: the strip lengths sum to 512; in every draw one strip holds 96 rows and one holds 32.
All inputs are finite; a program needn't handle non-finite values. No bound on the sum of `pixel_mask` on one device may be relied on, other than what follows from the above.
Results may differ from the reference program's by a relative error of at most 0.00098.
Values may be sent and summed in bfloat16 or wider, within the bound.
A program may use at most 192 MiB of HBM per device.

```python
import jax
import jax.numpy as jnp
from jax import lax

STOKES = 4
NW = 256
PARAMS = 9
RANK = 4
HALF = 32
MEAN_ROWS = 64
COLS = 256
TAPS = 65
CAP = 96
STRIPS = 8
ROWS = 512


def draw_unit_params(key, part):
    shape = (PARAMS, STRIPS, CAP * COLS)
    broad_key = jax.random.fold_in(key, 21)
    narrow_key = jax.random.fold_in(key, 22)
    broad = jax.random.uniform(broad_key, shape, jnp.float32, 0.0, 1.0)
    narrow = jax.random.uniform(narrow_key, shape, jnp.float32, 0.0, 1.0)
    narrow = 0.05 * narrow
    row_number = lax.broadcasted_iota(jnp.int32, shape, 0)
    is_narrow = (row_number == 4) | (row_number == 5)
    return jnp.where(is_narrow, narrow, broad).astype(jnp.float32)


def draw_strip_lengths(key, part):
    pair_count = STRIPS // 2
    first_key = jax.random.fold_in(key, 11)
    second_key = jax.random.fold_in(key, 12)
    third_key = jax.random.fold_in(key, 13)
    moved_rows = jax.random.randint(first_key, (pair_count,), -HALF, HALF + 1)
    chosen = jax.random.randint(second_key, (), 0, pair_count)
    moved_rows = jnp.where(jnp.arange(pair_count) == chosen, HALF, moved_rows).astype(jnp.int32)
    shuffled = jax.random.permutation(third_key, STRIPS)
    changes = jnp.zeros((STRIPS,), jnp.int32).at[shuffled[0::2]].add(moved_rows).at[shuffled[1::2]].add(-moved_rows)
    return (MEAN_ROWS + changes).astype(jnp.int32)


def with_ends(entries, key, low, high):
    longest = entries.shape.index(max(entries.shape))
    spots = []
    for shift in (0, 1):
        where = [jax.random.randint(jax.random.fold_in(key, axis), (), 0, length) for axis, length in enumerate(entries.shape)]
        where[longest] = (where[longest] + shift) % entries.shape[longest]
        spots.append(tuple(where))
    return entries.at[spots[0]].set(low).at[spots[1]].set(high)


def shard_levels(rng, dims, pieces, smallest, top_value):
    loudness, own = 1.0, jax.random.fold_in(rng, 6)
    for dim, blocks in pieces:
        steps = jnp.exp(jax.random.uniform(jax.random.fold_in(own, dim), (blocks,), jnp.float32, smallest / len(pieces), top_value / len(pieces)))
        loudness = loudness * jnp.repeat(steps, dims[dim] // blocks).reshape([-1 if axis == dim else 1 for axis in range(len(dims))])
    return loudness


def centred(rng, shape, width, limit, cuts=(), kind=jnp.bfloat16):
    entries = width * jax.random.normal(rng, shape, jnp.float32)
    if cuts:
        entries = entries * shard_levels(rng, shape, cuts, -0.22, 0.18)
    return jnp.clip(entries, -limit, limit).astype(kind)


def setup_inputs(seed: int = 0) -> dict:
    arg_keys = jax.random.split(jax.random.key(seed), 7)
    return {
        "unit_params": draw_unit_params(jax.random.fold_in(arg_keys[6], 71), 0),
        "observed": centred(arg_keys[1], (STOKES, NW, STRIPS * CAP, COLS), 0.5, 3.0, ((1, 4), (2, 8))),
        "psf_rows": centred(arg_keys[2], (NW, RANK, TAPS), TAPS ** -0.5, 0.75, ((0, 4),)),
        "psf_cols": centred(arg_keys[3], (NW, RANK, TAPS), TAPS ** -0.5, 0.75, ((0, 4),)),
        "pixel_mask": with_ends((jax.random.randint(arg_keys[4], (STRIPS * CAP, COLS), 0, 8) < 7).astype(jnp.int32), jax.random.fold_in(arg_keys[4], 1), 0, 1),
        "strip_lengths": draw_strip_lengths(jax.random.fold_in(arg_keys[6], 71), 0),
    }


parameter_low = (0.2, 0.4, 2.0, -0.8, 0.4, 0.3, 0.0, 0.0, 0.0)
parameter_span = (0.4, 0.6, 18.0, 1.6, 0.8, 1.2, 1.5, 3.141592653589793, 3.141592653589793)
stokes_weight = (1.0, 3.0, 3.0, 2.0)
loss_scale = 0.03125

def profile(distance, damping):
    scaled = distance / damping
    return 1.0 / (1.0 + scaled * scaled)

def stokes_model(unit_params, wave_grid):
    physical = [parameter_low[number] + parameter_span[number] * unit_params[number] for number in range(9)]
    source_zero, source_slope, strength, doppler, line_width, damping, zeeman_split, incline, azimuth = physical
    offset = (wave_grid[:, None, None] - doppler) / line_width
    split_ratio = zeeman_split / line_width
    centre = profile(offset, damping)
    upper_line = profile(offset - split_ratio, damping)
    lower_line = profile(offset + split_ratio, damping)
    cosine = jnp.cos(incline)
    sine_value = jnp.sin(incline)
    sine_square = sine_value * sine_value
    absorb_total = 1.0 + strength * (centre * sine_square * 0.5 + (upper_line + lower_line) * (1.0 + cosine * cosine) * 0.25)
    linear = strength * (centre - 0.5 * (upper_line + lower_line)) * sine_square * 0.5
    linear_cosine = linear * jnp.cos(2.0 * azimuth)
    linear_sine = linear * jnp.sin(2.0 * azimuth)
    circular = strength * (lower_line - upper_line) * cosine * 0.5
    denominator = absorb_total * absorb_total - linear_cosine * linear_cosine - linear_sine * linear_sine - circular * circular
    source_ratio = source_slope / denominator
    return jnp.stack([source_zero + source_ratio * absorb_total, -source_ratio * linear_cosine, -source_ratio * linear_sine, -source_ratio * circular])

def correlate(field, tap_table, axis_index):
    extent = field.shape[axis_index]
    tap_count = tap_table.shape[1]
    radius = tap_count // 2
    period = 1 << (extent + tap_count).bit_length()
    kernel = jnp.zeros((tap_table.shape[0], period), jnp.float32)
    kernel = kernel.at[:, :radius + 1].set(tap_table[:, radius:]).at[:, period - radius:].set(tap_table[:, :radius])
    kernel_spec = jnp.conj(jnp.fft.rfft(kernel, axis=1))
    layout = [tap_table.shape[0]] + [1] * (field.ndim - 1)
    layout[axis_index] = period // 2 + 1
    field_spec = jnp.fft.rfft(field, n=period, axis=axis_index)
    result = jnp.fft.irfft(field_spec * kernel_spec.reshape(layout), n=period, axis=axis_index)
    return lax.slice_in_dim(result, 0, extent, axis=axis_index)

def map_rows(strip_lengths):
    strip_ends = jnp.cumsum(strip_lengths).astype(jnp.int32)
    strip_starts = (strip_ends - strip_lengths).astype(jnp.int32)
    map_index = jnp.arange(ROWS, dtype=jnp.int32)
    owner_strip = lax.optimization_barrier(jnp.sum((map_index[:, None] >= strip_ends[None, :]).astype(jnp.int32), axis=1)).astype(jnp.int32)
    return (owner_strip * CAP + map_index - strip_starts[owner_strip]).astype(jnp.int32)

def reference(unit_params, observed, psf_rows, psf_cols, pixel_mask, strip_lengths):
    padded_rows = map_rows(strip_lengths)
    unit_map = unit_params.reshape(PARAMS, STRIPS * CAP, COLS)[:, padded_rows]
    live_map = pixel_mask[padded_rows].astype(jnp.float32)
    weight_square = jnp.array(stokes_weight, jnp.float32)
    weight_square = weight_square * weight_square

    def one_wave(number, gradient_sum):
        position = number.astype(jnp.float32)
        wave_grid = (-3.0 + 6.0 * position / (NW - 1)).reshape(1)

        def model_of(params_now):
            return stokes_model(params_now, wave_grid)[:, 0]
        model_exact, pullback = jax.vjp(model_of, unit_map)
        model_rounded = model_exact.astype(jnp.bfloat16)
        rows_taps = lax.dynamic_index_in_dim(psf_rows, number, 0, keepdims=False).astype(jnp.float32)
        cols_taps = lax.dynamic_index_in_dim(psf_cols, number, 0, keepdims=False).astype(jnp.float32)
        row_pass = correlate(model_rounded.astype(jnp.float32)[None], rows_taps, 2).astype(jnp.bfloat16)
        blurred = lax.optimization_barrier(jnp.sum(correlate(row_pass.astype(jnp.float32), cols_taps, 3), axis=0))
        observed_map = lax.dynamic_index_in_dim(observed, number, 1, keepdims=False)[:, padded_rows].astype(jnp.float32)
        residual = (loss_scale * weight_square[:, None, None] * live_map * (blurred - observed_map)).astype(jnp.bfloat16)
        across = correlate(residual.astype(jnp.float32)[None], cols_taps[:, ::-1], 3).astype(jnp.bfloat16)
        adjoint = lax.optimization_barrier(jnp.sum(correlate(across.astype(jnp.float32), rows_taps[:, ::-1], 2), axis=0))
        return gradient_sum + pullback(adjoint)[0]
    gradient_map = lax.fori_loop(0, NW, one_wave, jnp.zeros(unit_map.shape, jnp.float32))
    gradient_padded = jnp.zeros((PARAMS, STRIPS * CAP, COLS), jnp.float32).at[:, padded_rows].set(gradient_map)
    return gradient_padded.reshape(PARAMS, STRIPS, CAP * COLS)
```

```python
import functools

import jax
import jax.numpy as jnp
from jax import lax
from jax.experimental import pallas as pl
from jax.experimental.pallas import tpu as pltpu
from jax.sharding import PartitionSpec as P

parameter_low = (0.2, 0.4, 2.0, -0.8, 0.4, 0.3, 0.0, 0.0, 0.0)
parameter_span = (0.4, 0.6, 18.0, 1.6, 0.8, 1.2, 1.5, 3.141592653589793, 3.141592653589793)
stokes_weight = (1.0, 9.0, 9.0, 4.0)
loss_scale = 0.03125
lanes = 128


def passed_along(shard, axis, by):
    count = lax.axis_size(axis)
    pairs = [(i, i + by) for i in range(count) if 0 <= i + by < count]
    return lax.ppermute(shard, axis, pairs)


def swapped(shard, axis, step):
    count = lax.axis_size(axis)
    return lax.ppermute(shard, axis, [(i, i ^ step) for i in range(count)])


def physical_of(unit_params):
    return [
        parameter_low[number] + parameter_span[number] * unit_params[number] for number in range(9)
    ]


def inverse(value):
    guess = pl.reciprocal(value, approx=True)
    return guess * (2.0 - value * guess)


def circulant(taps, rows):
    wide = jnp.broadcast_to(taps, (rows, lanes))
    return pltpu.roll(wide, 0, 1, stride=1, stride_axis=0)


def kernel(
    grid_ref,
    const_ref,
    mask_ref,
    observed_ref,
    taps_ref,
    out_ref,
    model_ref,
    saved_ref,
    adjoint_ref,
    row_ref,
    back_ref,
    column_ref,
    pass_ref,
    residual_ref,
    across_ref,
):
    step = pl.program_id(0)
    steps = pl.num_programs(0)
    ranks = taps_ref.shape[1]
    stokes, _, rows, columns = observed_ref.shape
    wide = const_ref.shape[1]

    def model_chunk(slot, level, row, column):
        here = (pl.ds(row, 16), pl.ds(column, lanes))
        scale, shift, split, lin, tot, circ, zero, slope, cos2, sin2 = (
            const_ref[(number,) + here] for number in range(10)
        )
        z0 = level * scale - shift
        z1 = z0 - split
        z2 = z0 + split
        p0 = inverse(1.0 + z0 * z0)
        p1 = inverse(1.0 + z1 * z1)
        p2 = inverse(1.0 + z2 * z2)
        both = p1 + p2
        differ = p2 - p1
        absorb = 1.0 + lin * p0 + tot * both
        linear = lin * (p0 - 0.5 * both)
        circular = circ * differ
        inv = inverse(absorb * absorb - linear * linear - circular * circular)
        ratio = slope * inv
        polar = ratio * linear
        models = (zero + ratio * absorb, -(polar * cos2), -(polar * sin2), -(ratio * circular))
        for number in range(stokes):
            model_ref[(slot, number) + here] = models[number].astype(jnp.bfloat16)
        kept = (p0, both, differ, z0 * p0 * p0, z1 * p1 * p1, z2 * p2 * p2, absorb, inv)
        for number in range(8):
            saved_ref[(slot, number) + here] = kept[number]

    def pull_chunk(slot, level, row, column):
        here = (pl.ds(row, 16), pl.ds(column, lanes))
        p0, both, differ, y0, y1, y2, absorb, inv = (
            saved_ref[(slot, number) + here] for number in range(8)
        )
        lin, tot, circ = (const_ref[(number,) + here] for number in (3, 4, 5))
        slope, cos2, sin2 = (const_ref[(number,) + here] for number in (7, 8, 9))
        h0, h1, h2, h3 = (adjoint_ref[(slot, number) + here] for number in range(4))
        part = p0 - 0.5 * both
        linear = lin * part
        circular = circ * differ
        ratio = slope * inv
        along = h1 * cos2 + h2 * sin2
        turned = h2 * cos2 - h1 * sin2
        term = (h0 * absorb - along * linear - h3 * circular) * inv
        twice = term + term
        g_absorb = ratio * (h0 - twice * absorb)
        g_linear = ratio * (twice * linear - along)
        g_circular = ratio * (twice * circular - h3)
        g_both = tot * g_absorb - (0.5 * lin) * g_linear
        g_differ = circ * g_circular
        d1 = y1 * (g_both - g_differ)
        d2 = y2 * (g_both + g_differ)
        dz = y0 * (lin * (g_absorb + g_linear)) + d1 + d2
        sums = (
            h0,
            term,
            ratio * linear * turned,
            g_absorb * p0 + g_linear * part,
            g_absorb * both,
            g_circular * differ,
            dz,
            level * dz,
            d2 - d1,
        )
        for number in range(9):
            out_ref[(number,) + here] += sums[number]

    chunks = [(row, column) for row in range(0, wide, 16) for column in range(0, columns, lanes)]

    def chunk_loop(body, slot, level):
        def one(number, carry):
            row = pl.multiple_of(number * 16, 16)
            for column in range(0, columns, lanes):
                body(slot, level, row, column)
            return carry

        lax.fori_loop(0, wide // 16, one, 0)

    @pl.when(step == 0)
    def _():
        out_ref[...] = jnp.zeros_like(out_ref)
        saved_ref[1] = jnp.zeros(saved_ref.shape[1:], jnp.float32)
        adjoint_ref[1] = jnp.zeros(adjoint_ref.shape[1:], jnp.float32)
        model_ref[...] = jnp.zeros_like(model_ref)
        across_ref[...] = jnp.zeros_like(across_ref)
        column_ref[...] = jnp.zeros_like(column_ref)
        chunk_loop(model_chunk, 0, grid_ref[0])

    def tables(slot, rank):
        source = lax.broadcasted_iota(jnp.int32, (lanes, lanes), 0)
        target = lax.broadcasted_iota(jnp.int32, (lanes, lanes), 1)
        taps = taps_ref[slot, rank : rank + 1, :]
        ring = circulant(taps[:, :lanes], lanes)
        near = jnp.where(jnp.abs(source - target) <= 64, ring, 0.0).astype(jnp.bfloat16)
        after = jnp.where(source - target > 64, ring, 0.0).astype(jnp.bfloat16)
        before = jnp.where(target - source > 64, ring, 0.0).astype(jnp.bfloat16)
        base = rank * columns
        for block in range(columns // lanes):
            place = base + block * lanes
            column_ref[pl.ds(place, lanes), pl.ds(block * lanes, lanes)] = near
            if block > 0:
                column_ref[pl.ds(place, lanes), pl.ds((block - 1) * lanes, lanes)] = before
                column_ref[pl.ds(place - lanes, lanes), pl.ds(block * lanes, lanes)] = after
        ring = circulant(taps[:, lanes : 2 * lanes], rows)
        ahead = target[:rows] >= source[:rows]
        row_ref[pl.ds(rank * rows, rows), :lanes] = jnp.where(ahead, ring, 0.0).astype(jnp.bfloat16)
        row_ref[pl.ds(rank * rows, rows), lanes:] = jnp.where(ahead, 0.0, ring).astype(jnp.bfloat16)
        ring = circulant(taps[:, 2 * lanes :], lanes)
        inside = target <= source
        at = pl.ds(rank * lanes, lanes)
        back_ref[:lanes, at] = jnp.where(inside, ring, 0.0).astype(jnp.bfloat16)
        back_ref[lanes:, at] = jnp.where(inside, 0.0, ring)[: wide - lanes].astype(jnp.bfloat16)

    def row_piece(slot, number):
        product = jnp.dot(
            row_ref[...], model_ref[slot, number], preferred_element_type=jnp.float32
        ).astype(jnp.bfloat16)
        for rank in range(ranks):
            pass_ref[pl.ds(number * rows, rows), pl.ds(rank * columns, columns)] = product[
                rank * rows : (rank + 1) * rows
            ]

    def blur_piece(slot):
        blurred = jnp.dot(pass_ref[...], column_ref[...], preferred_element_type=jnp.float32)
        for number in range(stokes):
            seen = observed_ref[number, slot].astype(jnp.float32)
            gap = blurred[number * rows : (number + 1) * rows] - seen
            weighted = (stokes_weight[number] * mask_ref[...]) * gap
            residual_ref[pl.ds(number * rows, rows), :] = weighted.astype(jnp.bfloat16)

    def across_piece(rank):
        product = lax.dot_general(
            residual_ref[...],
            column_ref[pl.ds(rank * columns, columns), :],
            (((1,), (1,)), ((), ())),
            preferred_element_type=jnp.float32,
        ).astype(jnp.bfloat16)
        for number in range(stokes):
            across_ref[pl.ds(rank * lanes, rows), pl.ds(number * columns, columns)] = product[
                number * rows : (number + 1) * rows
            ]

    def adjoint_piece(slot, number):
        adjoint_ref[slot, number] = jnp.dot(
            back_ref[...],
            across_ref[:, pl.ds(number * columns, columns)],
            preferred_element_type=jnp.float32,
        )

    for slot in (0, 1):
        other = 1 - slot
        now = 2 * step + slot
        before_level = grid_ref[jnp.maximum(now - 1, 0)]
        after_level = grid_ref[now + 1]
        matrix = [functools.partial(tables, slot, rank) for rank in range(ranks)]
        matrix += [functools.partial(row_piece, slot, number) for number in range(stokes)]
        matrix += [functools.partial(blur_piece, slot)]
        matrix += [functools.partial(across_piece, rank) for rank in range(ranks)]
        matrix += [functools.partial(adjoint_piece, slot, number) for number in range(stokes)]
        vector = [functools.partial(pull_chunk, other, before_level, *at) for at in chunks]
        vector += [functools.partial(model_chunk, other, after_level, *at) for at in chunks]
        done = 0
        for number, piece in enumerate(matrix):
            piece()
            until = (number + 1) * len(vector) // len(matrix)
            for work in vector[done:until]:
                work()
            done = until

    @pl.when(step == steps - 1)
    def _():
        chunk_loop(pull_chunk, 1, grid_ref[2 * steps - 1])


def wave_sums(grid, consts, mask, observed, taps):
    stokes, waves, rows, columns = observed.shape
    ranks = taps.shape[1]
    wide = consts.shape[1]
    return pl.pallas_call(
        kernel,
        grid=(waves // 2,),
        out_shape=jax.ShapeDtypeStruct((9, wide, columns), jnp.float32),
        in_specs=[
            pl.BlockSpec(memory_space=pltpu.SMEM),
            pl.BlockSpec(consts.shape, lambda i: (0, 0, 0)),
            pl.BlockSpec(mask.shape, lambda i: (0, 0)),
            pl.BlockSpec((stokes, 2, rows, columns), lambda i: (0, i, 0, 0)),
            pl.BlockSpec((2,) + taps.shape[1:], lambda i: (i, 0, 0)),
        ],
        out_specs=pl.BlockSpec((9, wide, columns), lambda i: (0, 0, 0)),
        scratch_shapes=[
            pltpu.VMEM((2, stokes, 2 * lanes, columns), jnp.bfloat16),
            pltpu.VMEM((2, 8, wide, columns), jnp.float32),
            pltpu.VMEM((2, stokes, wide, columns), jnp.float32),
            pltpu.VMEM((ranks * rows, 2 * lanes), jnp.bfloat16),
            pltpu.VMEM((wide, ranks * lanes), jnp.bfloat16),
            pltpu.VMEM((ranks * columns, columns), jnp.bfloat16),
            pltpu.VMEM((stokes * rows, ranks * columns), jnp.bfloat16),
            pltpu.VMEM((stokes * rows, columns), jnp.bfloat16),
            pltpu.VMEM((ranks * lanes, stokes * columns), jnp.bfloat16),
        ],
        compiler_params=pltpu.CompilerParams(vmem_limit_bytes=48 * 1024 * 1024),
    )(grid, consts, mask, observed, taps)


def pixel_constants(params, live):
    zero, slope, strength, doppler, width, damping, split, incline, azimuth = physical_of(params)
    scale = 1.0 / (width * damping)
    cosine = jnp.cos(incline)
    sine = jnp.sin(incline)
    return jnp.stack(
        [
            scale,
            doppler * scale,
            split * scale,
            0.5 * strength * sine * sine,
            0.25 * strength * (1.0 + cosine * cosine),
            0.5 * strength * cosine,
            zero * live,
            slope * live,
            jnp.cos(2.0 * azimuth),
            jnp.sin(2.0 * azimuth),
        ]
    )


def unit_gradient(params, sums):
    _, _, strength, doppler, width, damping, split, incline, _ = physical_of(params)
    scale = 1.0 / (width * damping)
    cosine = jnp.cos(incline)
    sine = jnp.sin(incline)
    dz, dz_level, d_split = -2.0 * sums[6], -2.0 * sums[7], -2.0 * sums[8]
    d_scale = dz_level - doppler * dz + split * d_split
    physical = [
        sums[0],
        sums[1],
        0.5 * sine * sine * sums[3]
        + 0.25 * (1.0 + cosine * cosine) * sums[4]
        + 0.5 * cosine * sums[5],
        -scale * dz,
        -d_scale * scale / width,
        -d_scale * scale / damping,
        scale * d_split,
        strength * sine * (cosine * sums[3] - 0.5 * cosine * sums[4] - 0.5 * sums[5]),
        -2.0 * sums[2],
    ]
    return jnp.stack([parameter_span[number] * physical[number] for number in range(9)])


def per_device(unit_params, observed, psf_rows, psf_cols, pixel_mask, strip_lengths):
    stokes_count, wave_count, capacity, columns = observed.shape
    ranks, tap_count = psf_rows.shape[1:]
    radius = tap_count // 2
    wave_pos = lax.axis_index("wave")
    wave_total = lax.axis_size("wave")
    strip_pos = lax.axis_index("strip")
    strip_total = lax.axis_size("strip")
    length = strip_lengths[0]
    share = capacity // wave_total
    mine = unit_params.reshape(9, share, columns)

    others = [(wave_pos ^ step, swapped(mine, "wave", step)) for step in range(1, wave_total)]
    own = jnp.zeros((9, capacity, columns), jnp.float32)
    for place, block in [(wave_pos, mine)] + others:
        own = lax.dynamic_update_slice_in_dim(own, block, place * share, 1)
    tail = lax.dynamic_slice_in_dim(own, length - radius, radius, 1)
    upper = passed_along(tail, "strip", 1)
    lower = passed_along(own[:, :radius], "strip", -1)
    params = jnp.concatenate([upper, own, jnp.zeros_like(upper)], axis=1)
    params = lax.dynamic_update_slice_in_dim(params, lower, radius + length, 1)

    index = jnp.arange(capacity + 2 * radius, dtype=jnp.int32)
    live = (
        (index < radius) & (strip_pos > 0)
        | (index >= radius) & (index < radius + length)
        | (index >= radius + length)
        & (index < 2 * radius + length)
        & (strip_pos < strip_total - 1)
    )
    consts = pixel_constants(params, live.astype(jnp.float32)[:, None])
    rows_live = (jnp.arange(capacity, dtype=jnp.int32) < length)[:, None]
    mask = loss_scale * pixel_mask.astype(jnp.float32) * rows_live

    levels = (wave_pos * wave_count + jnp.arange(wave_count + 2, dtype=jnp.int32)).astype(
        jnp.float32
    )
    grid = -3.0 + 6.0 * levels / (wave_count * wave_total - 1)

    rows32 = psf_rows.astype(jnp.float32)
    cols32 = psf_cols.astype(jnp.float32)[:, :, ::-1]
    back32 = rows32[:, :, ::-1]
    gap = jnp.zeros((wave_count, ranks, lanes - tap_count), jnp.float32)
    taps = jnp.concatenate(
        [
            cols32[:, :, radius:],
            gap,
            cols32[:, :, :radius],
            rows32,
            gap,
            back32[:, :, tap_count - 1 :],
            gap,
            back32[:, :, : tap_count - 1],
        ],
        axis=2,
    )
    sums = wave_sums(grid, consts, mask, observed, taps)

    from_lower = passed_along(sums[:, :radius], "strip", -1)
    from_upper = passed_along(
        lax.dynamic_slice_in_dim(sums, radius + length, radius, 1), "strip", 1
    )
    total = jnp.where(rows_live, sums[:, radius : radius + capacity], 0.0)
    total = jnp.concatenate([total[:, :radius] + from_upper, total[:, radius:]], axis=1)
    ending = lax.dynamic_slice_in_dim(total, length - radius, radius, 1) + from_lower
    total = lax.dynamic_update_slice_in_dim(total, ending, length - radius, 1)

    def part(place):
        return lax.dynamic_slice_in_dim(total, place * share, share, 1)

    arrived = [swapped(part(wave_pos ^ step), "wave", step) for step in range(1, wave_total)]
    mine_sums = functools.reduce(jnp.add, arrived, part(wave_pos))
    return unit_gradient(mine, mine_sums).reshape(unit_params.shape)


def solution(mesh):
    return jax.shard_map(
        per_device,
        mesh=mesh,
        in_specs=(
            P(None, "strip", "wave"),
            P(None, "wave", "strip", None),
            P("wave", None, None),
            P("wave", None, None),
            P("strip", None),
            P("strip"),
        ),
        out_specs=P(None, "strip", "wave"),
        check_vma=False,
    )
```

```python
import functools

import jax
import jax.numpy as jnp
from jax import lax
from jax.experimental import pallas as pl
from jax.experimental.pallas import tpu as pltpu
from jax.sharding import PartitionSpec as P

parameter_low = (0.2, 0.4, 2.0, -0.8, 0.4, 0.3, 0.0, 0.0, 0.0)
parameter_span = (0.4, 0.6, 18.0, 1.6, 0.8, 1.2, 1.5, 3.141592653589793, 3.141592653589793)
stokes_weight = (1.0, 9.0, 9.0, 4.0)
loss_scale = 0.03125
lanes = 128


def passed_along(shard, axis, by):
    count = lax.axis_size(axis)
    pairs = [(i, i + by) for i in range(count) if 0 <= i + by < count]
    return lax.ppermute(shard, axis, pairs)


def swapped(shard, axis, step):
    count = lax.axis_size(axis)
    return lax.ppermute(shard, axis, [(i, i ^ step) for i in range(count)])


def physical_of(unit_params):
    return [
        parameter_low[number] + parameter_span[number] * unit_params[number] for number in range(9)
    ]


def inverse(value):
    guess = pl.reciprocal(value, approx=True)
    return guess * (2.0 - value * guess)


def circulant(taps, rows):
    wide = jnp.broadcast_to(taps, (rows, lanes))
    return pltpu.roll(wide, 0, 1, stride=1, stride_axis=0)


def kernel(
    grid_ref,
    const_ref,
    mask_ref,
    observed_ref,
    taps_ref,
    out_ref,
    model_ref,
    saved_ref,
    adjoint_ref,
    row_ref,
    back_ref,
    column_ref,
    pass_ref,
    residual_ref,
    across_ref,
):
    step = pl.program_id(0)
    steps = pl.num_programs(0)
    ranks = taps_ref.shape[1]
    stokes, _, rows, columns = observed_ref.shape
    wide = const_ref.shape[1]

    def model_chunk(pair, levels, row, column):
        here = (pl.ds(row, 16), pl.ds(column, lanes))
        scale, shift, split, lin, tot, circ, zero, slope, cos2, sin2 = (
            const_ref[(number,) + here] for number in range(10)
        )
        for slot, level in zip(pair, levels):
            z0 = level * scale - shift
            z1 = z0 - split
            z2 = z0 + split
            p0 = inverse(1.0 + z0 * z0)
            p1 = inverse(1.0 + z1 * z1)
            p2 = inverse(1.0 + z2 * z2)
            both = p1 + p2
            differ = p2 - p1
            absorb = 1.0 + lin * p0 + tot * both
            linear = lin * (p0 - 0.5 * both)
            circular = circ * differ
            inv = inverse(absorb * absorb - linear * linear - circular * circular)
            ratio = slope * inv
            polar = ratio * linear
            models = (zero + ratio * absorb, -(polar * cos2), -(polar * sin2), -(ratio * circular))
            for number in range(stokes):
                model_ref[(slot, number) + here] = models[number].astype(jnp.bfloat16)
            kept = (p0, both, differ, z0 * p0 * p0, z1 * p1 * p1, z2 * p2 * p2, absorb, inv)
            for number in range(8):
                saved_ref[(slot, number) + here] = kept[number]

    def pull_chunk(pair, levels, row, column):
        here = (pl.ds(row, 8), pl.ds(column, lanes))
        lin, tot, circ = (const_ref[(number,) + here] for number in (3, 4, 5))
        slope, cos2, sin2 = (const_ref[(number,) + here] for number in (7, 8, 9))
        totals = [out_ref[(number,) + here] for number in range(9)]
        for slot, level in zip(pair, levels):
            p0, both, differ, y0, y1, y2, absorb, inv = (
                saved_ref[(slot, number) + here] for number in range(8)
            )
            h0, h1, h2, h3 = (adjoint_ref[(slot, number) + here] for number in range(4))
            part = p0 - 0.5 * both
            linear = lin * part
            circular = circ * differ
            ratio = slope * inv
            along = h1 * cos2 + h2 * sin2
            turned = h2 * cos2 - h1 * sin2
            term = (h0 * absorb - along * linear - h3 * circular) * inv
            twice = term + term
            g_absorb = ratio * (h0 - twice * absorb)
            g_linear = ratio * (twice * linear - along)
            g_circular = ratio * (twice * circular - h3)
            g_both = tot * g_absorb - (0.5 * lin) * g_linear
            g_differ = circ * g_circular
            d1 = y1 * (g_both - g_differ)
            d2 = y2 * (g_both + g_differ)
            dz = y0 * (lin * (g_absorb + g_linear)) + d1 + d2
            sums = (
                h0,
                term,
                ratio * linear * turned,
                g_absorb * p0 + g_linear * part,
                g_absorb * both,
                g_circular * differ,
                dz,
                level * dz,
                d2 - d1,
            )
            totals = [total + added for total, added in zip(totals, sums)]
        for number in range(9):
            out_ref[(number,) + here] = totals[number]

    def tables(slot, wave, rank):
        source = lax.broadcasted_iota(jnp.int32, (lanes, lanes), 0)
        target = lax.broadcasted_iota(jnp.int32, (lanes, lanes), 1)
        taps = taps_ref[wave, rank : rank + 1, :]
        ring = circulant(taps[:, :lanes], lanes)
        near = jnp.where(jnp.abs(source - target) <= 64, ring, 0.0).astype(jnp.bfloat16)
        after = jnp.where(source - target > 64, ring, 0.0).astype(jnp.bfloat16)
        before = jnp.where(target - source > 64, ring, 0.0).astype(jnp.bfloat16)
        base = rank * columns
        for block in range(columns // lanes):
            place = base + block * lanes
            column_ref[slot, pl.ds(place, lanes), pl.ds(block * lanes, lanes)] = near
            if block > 0:
                column_ref[slot, pl.ds(place, lanes), pl.ds((block - 1) * lanes, lanes)] = before
                column_ref[slot, pl.ds(place - lanes, lanes), pl.ds(block * lanes, lanes)] = after
        ring = circulant(taps[:, lanes : 2 * lanes], rows)
        ahead = target[:rows] >= source[:rows]
        at = pl.ds(rank * rows, rows)
        row_ref[slot, at, :lanes] = jnp.where(ahead, ring, 0.0).astype(jnp.bfloat16)
        row_ref[slot, at, lanes:] = jnp.where(ahead, 0.0, ring).astype(jnp.bfloat16)
        ring = circulant(taps[:, 2 * lanes :], lanes)
        inside = target <= source
        at = pl.ds(rank * lanes, lanes)
        back_ref[slot, :lanes, at] = jnp.where(inside, ring, 0.0).astype(jnp.bfloat16)
        rest = jnp.where(inside, 0.0, ring)[: wide - lanes]
        back_ref[slot, lanes:, at] = rest.astype(jnp.bfloat16)

    def row_piece(slot, number):
        product = jnp.dot(
            row_ref[slot], model_ref[slot, number], preferred_element_type=jnp.float32
        ).astype(jnp.bfloat16)
        for rank in range(ranks):
            pass_ref[slot % 2, pl.ds(number * rows, rows), pl.ds(rank * columns, columns)] = (
                product[rank * rows : (rank + 1) * rows]
            )

    def blur_piece(slot):
        blurred = jnp.dot(
            pass_ref[slot % 2], column_ref[slot], preferred_element_type=jnp.float32
        )
        for number in range(stokes):
            seen = observed_ref[number, slot].astype(jnp.float32)
            gap = blurred[number * rows : (number + 1) * rows] - seen
            weighted = (stokes_weight[number] * mask_ref[...]) * gap
            residual_ref[slot % 2, pl.ds(number * rows, rows), :] = weighted.astype(jnp.bfloat16)

    def across_piece(slot, rank):
        product = lax.dot_general(
            residual_ref[slot % 2],
            column_ref[slot, pl.ds(rank * columns, columns), :],
            (((1,), (1,)), ((), ())),
            preferred_element_type=jnp.float32,
        ).astype(jnp.bfloat16)
        for number in range(stokes):
            across_ref[slot % 2, pl.ds(rank * lanes, rows), pl.ds(number * columns, columns)] = (
                product[number * rows : (number + 1) * rows]
            )

    def adjoint_piece(slot, number):
        adjoint_ref[slot, number] = jnp.dot(
            back_ref[slot],
            across_ref[slot % 2, :, pl.ds(number * columns, columns)],
            preferred_element_type=jnp.float32,
        )

    def levels_at(wave):
        return [grid_ref[wave], grid_ref[wave + 1]]

    def strip_loop(body, height, pair, levels):
        def one(number, carry):
            row = pl.multiple_of(number * height, height)
            for column in range(0, columns, lanes):
                body(pair, levels, row, column)
            return carry

        lax.fori_loop(0, wide // height, one, 0)

    @pl.when(step == 0)
    def _():
        out_ref[...] = jnp.zeros_like(out_ref)
        saved_ref[2:] = jnp.zeros((2,) + saved_ref.shape[1:], jnp.float32)
        adjoint_ref[2:] = jnp.zeros((2,) + adjoint_ref.shape[1:], jnp.float32)
        model_ref[...] = jnp.zeros_like(model_ref)
        across_ref[...] = jnp.zeros_like(across_ref)
        column_ref[...] = jnp.zeros_like(column_ref)
        strip_loop(model_chunk, 16, (0, 1), levels_at(0))
        for slot in (0, 1):
            for rank in range(ranks):
                tables(slot, slot, rank)

    for half in (0, 1):
        pair = (2 * half, 2 * half + 1)
        other = (2 - 2 * half, 3 - 2 * half)
        now = 4 * step + 2 * half
        earlier = levels_at(jnp.maximum(now - 2, 0))
        later = levels_at(now + 2)
        matrix = []
        for number in range(stokes):
            matrix += [(1, functools.partial(row_piece, slot, number)) for slot in pair]
        matrix += [(4, functools.partial(blur_piece, slot)) for slot in pair]
        for rank in range(ranks):
            matrix += [(1, functools.partial(across_piece, slot, rank)) for slot in pair]
        for number in range(stokes):
            matrix += [(1, functools.partial(adjoint_piece, slot, number)) for slot in pair]
        vector = []
        for row in range(0, wide, 16):
            for column in range(0, columns, lanes):
                vector += [functools.partial(pull_chunk, other, earlier, row, column)]
                vector += [functools.partial(pull_chunk, other, earlier, row + 8, column)]
                vector += [functools.partial(model_chunk, other, later, row, column)]
        count = len(vector) // (2 * ranks)
        for number in range(2 * ranks):
            slot, rank = number % 2, number // 2
            vector.insert(
                (count + 1) * number, functools.partial(tables, other[slot], now + 2 + slot, rank)
            )
        whole = sum(weight for weight, _ in matrix)
        done = passed = 0
        for weight, piece in matrix:
            piece()
            passed += weight
            until = passed * len(vector) // whole
            for work in vector[done:until]:
                work()
            done = until

    @pl.when(step == steps - 1)
    def _():
        strip_loop(pull_chunk, 8, (2, 3), levels_at(4 * steps - 2))


def wave_sums(grid, consts, mask, observed, taps):
    stokes, waves, rows, columns = observed.shape
    ranks = taps.shape[1]
    wide = consts.shape[1]
    return pl.pallas_call(
        kernel,
        grid=(waves // 4,),
        out_shape=jax.ShapeDtypeStruct((9, wide, columns), jnp.float32),
        in_specs=[
            pl.BlockSpec(memory_space=pltpu.SMEM),
            pl.BlockSpec(consts.shape, lambda i: (0, 0, 0)),
            pl.BlockSpec(mask.shape, lambda i: (0, 0)),
            pl.BlockSpec((stokes, 4, rows, columns), lambda i: (0, i, 0, 0)),
            pl.BlockSpec(taps.shape, lambda i: (0, 0, 0)),
        ],
        out_specs=pl.BlockSpec((9, wide, columns), lambda i: (0, 0, 0)),
        scratch_shapes=[
            pltpu.VMEM((4, stokes, 2 * lanes, columns), jnp.bfloat16),
            pltpu.VMEM((4, 8, wide, columns), jnp.float32),
            pltpu.VMEM((4, stokes, wide, columns), jnp.float32),
            pltpu.VMEM((4, ranks * rows, 2 * lanes), jnp.bfloat16),
            pltpu.VMEM((4, wide, ranks * lanes), jnp.bfloat16),
            pltpu.VMEM((4, ranks * columns, columns), jnp.bfloat16),
            pltpu.VMEM((2, stokes * rows, ranks * columns), jnp.bfloat16),
            pltpu.VMEM((2, stokes * rows, columns), jnp.bfloat16),
            pltpu.VMEM((2, ranks * lanes, stokes * columns), jnp.bfloat16),
        ],
        compiler_params=pltpu.CompilerParams(vmem_limit_bytes=56 * 1024 * 1024),
    )(grid, consts, mask, observed, taps)


def pixel_constants(params, live):
    zero, slope, strength, doppler, width, damping, split, incline, azimuth = physical_of(params)
    scale = 1.0 / (width * damping)
    cosine = jnp.cos(incline)
    sine = jnp.sin(incline)
    return jnp.stack(
        [
            scale,
            doppler * scale,
            split * scale,
            0.5 * strength * sine * sine,
            0.25 * strength * (1.0 + cosine * cosine),
            0.5 * strength * cosine,
            zero * live,
            slope * live,
            jnp.cos(2.0 * azimuth),
            jnp.sin(2.0 * azimuth),
        ]
    )


def unit_gradient(params, sums):
    _, _, strength, doppler, width, damping, split, incline, _ = physical_of(params)
    scale = 1.0 / (width * damping)
    cosine = jnp.cos(incline)
    sine = jnp.sin(incline)
    dz, dz_level, d_split = -2.0 * sums[6], -2.0 * sums[7], -2.0 * sums[8]
    d_scale = dz_level - doppler * dz + split * d_split
    physical = [
        sums[0],
        sums[1],
        0.5 * sine * sine * sums[3]
        + 0.25 * (1.0 + cosine * cosine) * sums[4]
        + 0.5 * cosine * sums[5],
        -scale * dz,
        -d_scale * scale / width,
        -d_scale * scale / damping,
        scale * d_split,
        strength * sine * (cosine * sums[3] - 0.5 * cosine * sums[4] - 0.5 * sums[5]),
        -2.0 * sums[2],
    ]
    return jnp.stack([parameter_span[number] * physical[number] for number in range(9)])


def per_device(unit_params, observed, psf_rows, psf_cols, pixel_mask, strip_lengths):
    stokes_count, wave_count, capacity, columns = observed.shape
    ranks, tap_count = psf_rows.shape[1:]
    radius = tap_count // 2
    wave_pos = lax.axis_index("wave")
    wave_total = lax.axis_size("wave")
    strip_pos = lax.axis_index("strip")
    strip_total = lax.axis_size("strip")
    length = strip_lengths[0]
    share = capacity // wave_total
    mine = unit_params.reshape(9, share, columns)

    others = [(wave_pos ^ step, swapped(mine, "wave", step)) for step in range(1, wave_total)]
    own = jnp.zeros((9, capacity, columns), jnp.float32)
    for place, block in [(wave_pos, mine)] + others:
        own = lax.dynamic_update_slice_in_dim(own, block, place * share, 1)
    tail = lax.dynamic_slice_in_dim(own, length - radius, radius, 1)
    upper = passed_along(tail, "strip", 1)
    lower = passed_along(own[:, :radius], "strip", -1)
    index = jnp.arange(capacity + 2 * radius, dtype=jnp.int32)
    live = (
        (index < radius) & (strip_pos > 0)
        | (index >= radius) & (index < radius + length)
        | (index >= radius + length)
        & (index < 2 * radius + length)
        & (strip_pos < strip_total - 1)
    )
    wide = capacity + 2 * radius
    padded = jnp.pad(lower, ((0, 0), (capacity + radius, capacity - radius), (0, 0)))
    placed = lax.dynamic_slice_in_dim(padded, capacity - length, wide, 1)
    middle = jnp.pad(own, ((0, 0), (radius, radius), (0, 0)))
    first = jnp.pad(upper, ((0, 0), (0, wide - radius), (0, 0)))
    column_index = index[:, None]
    params = jnp.where(
        column_index < radius, first, jnp.where(column_index < radius + length, middle, placed)
    )
    consts = pixel_constants(params, live.astype(jnp.float32)[:, None])
    rows_live = (jnp.arange(capacity, dtype=jnp.int32) < length)[:, None]
    mask = loss_scale * pixel_mask.astype(jnp.float32) * rows_live

    levels = (wave_pos * wave_count + jnp.arange(wave_count + 4, dtype=jnp.int32)).astype(
        jnp.float32
    )
    grid = -3.0 + 6.0 * levels / (wave_count * wave_total - 1)

    rows32 = psf_rows.astype(jnp.float32)
    cols32 = psf_cols.astype(jnp.float32)[:, :, ::-1]
    back32 = rows32[:, :, ::-1]
    gap = jnp.zeros((wave_count, ranks, lanes - tap_count), jnp.float32)
    taps = jnp.concatenate(
        [
            cols32[:, :, radius:],
            gap,
            cols32[:, :, :radius],
            rows32,
            gap,
            back32[:, :, tap_count - 1 :],
            gap,
            back32[:, :, : tap_count - 1],
        ],
        axis=2,
    )
    taps = jnp.pad(taps, ((0, 4), (0, 0), (0, 0)))
    sums = wave_sums(grid, consts, mask, observed, taps)

    from_lower = passed_along(sums[:, :radius], "strip", -1)
    from_upper = passed_along(
        lax.dynamic_slice_in_dim(sums, radius + length, radius, 1), "strip", 1
    )
    total = jnp.where(rows_live, sums[:, radius : radius + capacity], 0.0)
    padded = jnp.pad(from_lower, ((0, 0), (capacity - radius,) * 2, (0, 0)))
    placed = lax.dynamic_slice_in_dim(padded, capacity - length, capacity, 1)
    total = total + placed + jnp.pad(from_upper, ((0, 0), (0, capacity - radius), (0, 0)))

    def part(place):
        return lax.dynamic_slice_in_dim(total, place * share, share, 1)

    arrived = [swapped(part(wave_pos ^ step), "wave", step) for step in range(1, wave_total)]
    mine_sums = functools.reduce(jnp.add, arrived, part(wave_pos))
    return unit_gradient(mine, mine_sums).reshape(unit_params.shape)


def solution(mesh):
    return jax.shard_map(
        per_device,
        mesh=mesh,
        in_specs=(
            P(None, "strip", "wave"),
            P(None, "wave", "strip", None),
            P("wave", None, None),
            P("wave", None, None),
            P("strip", None),
            P("strip"),
        ),
        out_specs=P(None, "strip", "wave"),
        check_vma=False,
    )
```
